256 devices in a mesh: row: 32 (over z, y_hi, core), col: 8 (over x, y_lo).
Axes of the slice: x: 4, y: 4 (y_hi: 2, y_lo: 2; y = y_hi * 2 + y_lo), z: 8, core: 2. Of those that a mesh axis runs over, the one named last changes fastest.
Arguments:
- rewards: float32 [16384, 512], P(('row', 'col')), as said below
- tile_data: bfloat16 [32, 8, 12, 256, 256], P('row', 'col'), as said below
- tile_slots: int32 [32, 8, 12], P('row', 'col'), may hold values from 0 to 15, as said below
- tile_count: int32 [32, 8], P('row', 'col'), may hold values from 6 to 12, as said below
Outputs:
- estimate: float32 [16384, 512], P(('row', 'col'))
- relative_residual: float32 [512], replicated
The draws below stay inside these ranges and needn't reach their ends.
Inputs may be any that keep to these rules, and one draw needn't show every extreme that they name: rewards have a scale per state and a scale per channel. `tile_data`: entries are nonnegative; every row of P sums to at most 1. `tile_slots`: in every block, slot s lies in tile row (s + a start drawn per block) mod 2. `tile_count`: some block has all 12 slots live.
All inputs are finite; a program needn't handle non-finite values.
Results may differ from the reference program's by a relative error of at most 0.00043.
Values may be sent and summed in bfloat16 or wider, within the bound.
No kernel may reach another device: no remote copies, remote signals or barrier semaphores. Data moves between devices by JAX's collectives and lax.ppermute only.
A program may use at most 128 MiB of HBM per device.

```python
import math
import jax
import jax.numpy as jnp
from jax import lax

CHANNELS = 512
TILE = 256
STATES_DEV = 64
TILES_DEV = 12
ITERS = 2
ROW_BLOCKS = 32
COL_BLOCKS = 8
STATES = 16384
TILE_ROWS = 2
TILE_COLS = 8


def shared_layout(key):
    base_key = jax.random.fold_in(key, 101)
    key_counts, key_chosen, key_start, key_cols = jax.random.split(base_key, 4)
    counts = jax.random.randint(key_counts, (ROW_BLOCKS * COL_BLOCKS,), TILES_DEV // 2, TILES_DEV + 1, jnp.int32)
    chosen = jax.random.randint(key_chosen, (), 0, ROW_BLOCKS * COL_BLOCKS, jnp.int32)
    counts = counts.at[chosen].set(TILES_DEV)
    counts = counts.reshape(ROW_BLOCKS, COL_BLOCKS).astype(jnp.int32)
    start = jax.random.randint(key_start, (ROW_BLOCKS * COL_BLOCKS, 1), 0, TILE_ROWS, jnp.int32)
    start = start.at[chosen, 0].set(TILE_ROWS - 1)
    start = start.reshape(ROW_BLOCKS, COL_BLOCKS, 1)
    slot_index = jnp.arange(TILES_DEV, dtype=jnp.int32)
    tile_row = (slot_index[None, None, :] + start) % TILE_ROWS
    tile_col = jax.random.randint(key_cols, (ROW_BLOCKS * COL_BLOCKS, TILES_DEV), 0, TILE_COLS, jnp.int32)
    tile_col = tile_col.at[chosen, 0].set(TILE_COLS - 1)
    tile_col = tile_col.at[chosen, 1].set(0)
    tile_col = tile_col.reshape(ROW_BLOCKS, COL_BLOCKS, TILES_DEV)
    slots = (tile_row * TILE_COLS + tile_col).astype(jnp.int32)
    return (counts, slots)


def draw_rewards(key, part):
    key = jax.random.fold_in(key, 11)
    key_rows, key_chan, key_base = jax.random.split(key, 3)
    row_scale = jnp.exp(jax.random.uniform(key_rows, (STATES, 1), jnp.float32, 0.0, math.log(10.0))) / 3.0
    chan_scale = jnp.exp(jax.random.uniform(key_chan, (1, CHANNELS), jnp.float32, -1.15, 1.15))
    base_draw = jax.random.normal(key_base, (STATES, CHANNELS), jnp.float32)
    return (base_draw * row_scale * chan_scale).astype(jnp.float32)


def draw_tile_data(key, part):
    counts, slots = shared_layout(key)
    key = jax.random.fold_in(key, 5)
    key_cols, key_exps, key_stay = jax.random.split(key, 3)
    targets = jax.random.randint(key_cols, (ROW_BLOCKS, COL_BLOCKS, TILES_DEV, TILE, 2), 0, TILE, jnp.int32)
    powers = jax.random.randint(key_exps, (ROW_BLOCKS, COL_BLOCKS, TILES_DEV, TILE, 2), 0, 16, jnp.int32)
    weights = jnp.left_shift(jnp.ones((), jnp.int32), powers)
    row_weight = jnp.sum(weights, axis=-1)
    tile_row = slots // TILE_COLS
    onehot = (tile_row[..., None] == jnp.arange(TILE_ROWS, dtype=jnp.int32)).astype(jnp.int32)
    totals = jnp.sum(onehot[..., None] * row_weight[:, :, :, None, :], axis=(1, 2))
    stay = jax.random.uniform(key_stay, (ROW_BLOCKS, TILE_ROWS, TILE), jnp.float32, 0.6, 1.0)
    scale = stay / jnp.maximum(totals, 1).astype(jnp.float32)
    scale_slot = jnp.sum(onehot[..., None].astype(jnp.float32) * scale[:, None, None, :, :], axis=3)
    values = weights.astype(jnp.float32) * scale_slot[..., None]
    columns = jnp.arange(TILE, dtype=jnp.int32)
    tile = jnp.where(targets[..., 0, None] == columns, values[..., 0, None], 0.0)
    tile = tile + jnp.where(targets[..., 1, None] == columns, values[..., 1, None], 0.0)
    return tile.astype(jnp.bfloat16)


def draw_tile_slots(key, part):
    counts, slots = shared_layout(key)
    return slots


def draw_tile_count(key, part):
    counts, slots = shared_layout(key)
    return counts


def setup_inputs(seed: int = 0) -> dict:
    streams_of = jax.random.split(jax.random.key(seed), 5)
    return {
        "rewards": draw_rewards(jax.random.fold_in(streams_of[4], 71), 0),
        "tile_data": draw_tile_data(jax.random.fold_in(streams_of[4], 71), 0),
        "tile_slots": draw_tile_slots(jax.random.fold_in(streams_of[4], 71), 0),
        "tile_count": draw_tile_count(jax.random.fold_in(streams_of[4], 71), 0),
    }


EPS = 1e-06
GAMMA = 0.9

def forward_part(tile_data, tile_slots, tile_count, values_block):
    n_slots = tile_data.shape[0]
    tile_size = tile_data.shape[-1]
    pieces = values_block.reshape(TILE_COLS, tile_size, -1)[tile_slots % TILE_COLS]
    products = jnp.einsum('sij,sjk->sik', tile_data.astype(jnp.float32), pieces.astype(jnp.float32), precision=lax.Precision.HIGHEST)
    live_mask = (jnp.arange(n_slots, dtype=jnp.int32) < tile_count).astype(jnp.float32)
    placing = (tile_slots[None, :] // TILE_COLS == jnp.arange(TILE_ROWS, dtype=jnp.int32)[:, None]).astype(jnp.float32) * live_mask[None, :]
    return jnp.einsum('ts,sik->tik', placing, products, precision=lax.Precision.HIGHEST).reshape(TILE_ROWS * tile_size, -1)

def backward_part(tile_data, tile_slots, tile_count, values_block):
    n_slots = tile_data.shape[0]
    tile_size = tile_data.shape[-1]
    pieces = values_block.reshape(TILE_ROWS, tile_size, -1)[tile_slots // TILE_COLS]
    products = jnp.einsum('sij,sik->sjk', tile_data.astype(jnp.float32), pieces.astype(jnp.float32), precision=lax.Precision.HIGHEST)
    live_mask = (jnp.arange(n_slots, dtype=jnp.int32) < tile_count).astype(jnp.float32)
    placing = (tile_slots[None, :] % TILE_COLS == jnp.arange(TILE_COLS, dtype=jnp.int32)[:, None]).astype(jnp.float32) * live_mask[None, :]
    return jnp.einsum('ts,sjk->tjk', placing, products, precision=lax.Precision.HIGHEST).reshape(TILE_COLS * tile_size, -1)

def channel_norm(values):
    return jnp.sqrt(lax.optimization_barrier(jnp.sum(values * values, axis=0)) + EPS)

def reference(rewards, tile_data, tile_slots, tile_count):

    def apply_forward(right_vec):
        rounded = right_vec.astype(jnp.bfloat16)
        columns = rounded.reshape(ROW_BLOCKS, COL_BLOCKS, STATES_DEV, CHANNELS).transpose(1, 0, 2, 3)
        columns = columns.reshape(COL_BLOCKS, ROW_BLOCKS * STATES_DEV, CHANNELS)

        def row_block_sum(pieces):
            return lax.optimization_barrier(jnp.sum(jax.vmap(forward_part)(pieces[0], pieces[1], pieces[2], columns), axis=0))
        summed = lax.map(row_block_sum, (tile_data, tile_slots, tile_count))
        return right_vec - GAMMA * summed.reshape(STATES, CHANNELS)

    def apply_adjoint(left_vec):
        rounded = left_vec.astype(jnp.bfloat16)
        row_blocks = rounded.reshape(ROW_BLOCKS, COL_BLOCKS * STATES_DEV, CHANNELS)

        def col_block_sum(pieces):
            partials = jax.vmap(backward_part)(pieces[0], pieces[1], pieces[2], row_blocks)
            return lax.optimization_barrier(jnp.sum(-GAMMA * partials, axis=0))
        summed = lax.map(col_block_sum, (tile_data.transpose(1, 0, 2, 3, 4), tile_slots.transpose(1, 0, 2), tile_count.T))
        summed = summed.reshape(COL_BLOCKS, ROW_BLOCKS, STATES_DEV, CHANNELS).transpose(1, 0, 2, 3).reshape(STATES, CHANNELS)
        return left_vec + summed
    beta_val = channel_norm(rewards)
    beta_first = beta_val
    left_vec = rewards / beta_val
    raw_vec = apply_adjoint(left_vec)
    alpha_val = channel_norm(raw_vec)
    right_vec = raw_vec / alpha_val
    direction = right_vec
    estimate = jnp.zeros((STATES, CHANNELS), jnp.float32)
    phibar = beta_val
    rhobar = alpha_val
    for iteration in range(ITERS):
        left_vec = apply_forward(right_vec) - alpha_val * left_vec
        beta_val = channel_norm(left_vec)
        left_vec = left_vec / beta_val
        raw_vec = apply_adjoint(left_vec) - beta_val * right_vec
        alpha_val = channel_norm(raw_vec)
        right_vec = raw_vec / alpha_val
        rho_val = jnp.sqrt(rhobar * rhobar + beta_val * beta_val)
        cosine = rhobar / rho_val
        sine_val = beta_val / rho_val
        theta_val = sine_val * alpha_val
        rhobar = -cosine * alpha_val
        phi_val = cosine * phibar
        phibar = sine_val * phibar
        estimate = estimate + phi_val / rho_val * direction
        direction = right_vec - theta_val / rho_val * direction
    return (estimate, phibar / beta_first)
```

```python
import functools

import jax
import jax.numpy as jnp
import numpy as np
from jax import lax
from jax.experimental import pallas as pl
from jax.experimental.pallas import tpu as pltpu
from jax.sharding import Mesh, PartitionSpec as P

ITERS = 2
EPS = 1e-06
GAMMA = 0.9

AXES = ("z", "yh", "core", "x", "yl")
SIZES = (8, 2, 2, 4, 2)
ROWS = ("z", "yh")
COLS = ("x", "yl")
N_ROWS = 16
N_COLS = 8
TILE = 256
STATES_DEV = 64
PAIR = 2 * STATES_DEV
CHANS = 256
SLOTS = 12
TILE_COLS = 8
HEAD = 16
MSG = PAIR + HEAD
BITS = 14.0
BF16 = jnp.bfloat16
F32 = jnp.float32
I16 = jnp.int16


def to_i16(values):
    return values.astype(jnp.int32).astype(I16)


def scaled_exponent(largest):
    return jnp.ceil(jnp.log2(jnp.maximum(largest, 1e-30)))


def head_rows(exponent, square):
    square_exp = scaled_exponent(square)
    mantissa = square * jnp.exp2(-square_exp) * 16384.0
    high = jnp.round(mantissa)
    low = jnp.round((mantissa - high) * 16384.0)
    row = lax.broadcasted_iota(jnp.int32, (HEAD, exponent.shape[-1]), 0)
    rows = jnp.where(row == 0, exponent, jnp.where(row == 1, square_exp, jnp.where(row == 2, high, low)))
    return to_i16(rows)


def read_head(head):
    rows = head.astype(jnp.int32).astype(F32)
    step = jnp.exp2(rows[0:1] - BITS)
    square = (rows[2:3] + rows[3:4] * (1.0 / 16384.0)) * (1.0 / 16384.0) * jnp.exp2(rows[1:2])
    return step, square


def quantized(block):
    exponent = scaled_exponent(jnp.max(jnp.abs(block), axis=0, keepdims=True))
    return to_i16(jnp.round(block * jnp.exp2(BITS - exponent))), exponent


def store_message(out_ref, block, square):
    values, exponent = quantized(block)
    head = head_rows(exponent, square)
    for i in range(out_ref.shape[0]):
        out_ref[i, :PAIR, :] = values
        out_ref[i, PAIR:, :] = head


def wide(values):
    return values.astype(jnp.int32).astype(F32)


def split_store(ref, index, rows, values):
    high = values.astype(BF16)
    ref[index, rows, :CHANS] = high
    ref[index, rows, CHANS:] = (values - high.astype(F32)).astype(BF16)


def forward_kernel(meta_ref, msg_ref, own_ref, other_ref, out_ref, vec_ref, sum_ref):
    square = jnp.zeros((1, CHANS), F32)
    for k in range(N_ROWS):
        step, part = read_head(msg_ref[k, PAIR:, :])
        square = square + part
        split_store(vec_ref, k // 2, pl.ds((k % 2) * PAIR, PAIR), wide(msg_ref[k, :PAIR, :]) * step)
    core = meta_ref[2, 0]
    for which, tiles_ref in enumerate((own_ref, other_ref)):
        at_core = core if which == 0 else 1 - core
        count = meta_ref[which, SLOTS]
        start = meta_ref[which, 0] // TILE_COLS
        for parity in range(2):
            total = jnp.zeros((TILE, 2 * CHANS), F32)
            for s in range(parity, SLOTS, 2):
                live = jnp.where(s < count, 1.0, 0.0).astype(F32)
                vec = vec_ref[meta_ref[which, s] % TILE_COLS]
                total = total + live * jnp.dot(tiles_ref[s], vec, preferred_element_type=F32)
            tile_row = (start + parity) % 2
            summed = total[:, :CHANS] + total[:, CHANS:]
            for q in range(4):
                sum_ref[tile_row * 4 + q, pl.ds(at_core * STATES_DEV, STATES_DEV), :] = summed[
                    q * STATES_DEV : (q + 1) * STATES_DEV
                ]
    for k in range(N_COLS):
        values, exponent = quantized(sum_ref[k])
        out_ref[k, :PAIR, :] = values
        out_ref[k, PAIR:, :] = head_rows(exponent, square)


def adjoint_kernel(meta_ref, msg_ref, own_ref, other_ref, out_ref, vec_ref, sum_ref):
    square = jnp.zeros((1, CHANS), F32)
    for k in range(N_COLS):
        step, part = read_head(msg_ref[k, PAIR:, :])
        square = square + part
        for core in range(2):
            values = wide(msg_ref[k, core * STATES_DEV : (core + 1) * STATES_DEV, :]) * step
            split_store(vec_ref, core * 2 + k // 4, pl.ds((k % 4) * STATES_DEV, STATES_DEV), values)
    sum_ref[...] = jnp.zeros_like(sum_ref)
    core = meta_ref[2, 0]
    for which, tiles_ref in enumerate((own_ref, other_ref)):
        at_core = core if which == 0 else 1 - core
        count = meta_ref[which, SLOTS]
        for s in range(SLOTS):
            slot = meta_ref[which, s]

            @pl.when(s < count)
            def _():
                vec = vec_ref[at_core * 2 + slot // TILE_COLS]
                product = lax.dot_general(
                    tiles_ref[s], vec, (((0,), (0,)), ((), ())), preferred_element_type=F32
                )
                sum_ref[slot % TILE_COLS] += product[:, :CHANS] + product[:, CHANS:]

    for k in range(N_ROWS):
        values, exponent = quantized(sum_ref[k // 2, (k % 2) * PAIR : (k % 2 + 1) * PAIR, :])
        out_ref[k, :PAIR, :] = values
        out_ref[k, PAIR:, :] = head_rows(exponent, square)


def summed_messages(msg_ref):
    total = jnp.zeros((PAIR, CHANS), F32)
    square = jnp.zeros((1, CHANS), F32)
    for k in range(msg_ref.shape[0]):
        step, part = read_head(msg_ref[k, PAIR:, :])
        total = total + wide(msg_ref[k, :PAIR, :]) * step
        square = square + part
    return total, square


def first_kernel(rewards_ref, out_ref):
    rewards = rewards_ref[...]
    store_message(out_ref, rewards, jnp.sum(rewards * rewards, axis=0, keepdims=True))


def adjoint_end_kernel(first, msg_ref, left_ref, *refs):
    right_ref, (raw_ref, unit_ref, norm_ref, out_ref) = (None, refs) if first else (refs[0], refs[1:])
    total, square = summed_messages(msg_ref)
    beta = jnp.sqrt(square + EPS)
    unit = left_ref[...] / beta
    raw = unit - GAMMA * (total / beta)
    if not first:
        raw = raw - beta * right_ref[...]
    raw_ref[...] = raw
    unit_ref[...] = unit
    norm_ref[...] = jnp.broadcast_to(beta, norm_ref.shape)
    store_message(out_ref, raw, jnp.sum(raw * raw, axis=0, keepdims=True))


def forward_end_kernel(msg_ref, raw_ref, unit_ref, left_ref, right_ref, norm_ref, square_ref, out_ref):
    total, square = summed_messages(msg_ref)
    alpha = jnp.sqrt(square + EPS)
    right = raw_ref[...] / alpha
    left = right - GAMMA * (total / alpha) - alpha * unit_ref[...]
    left_ref[...] = left
    right_ref[...] = right
    norm_ref[...] = jnp.broadcast_to(alpha, norm_ref.shape)
    own = jnp.sum(left * left, axis=0, keepdims=True)
    square_ref[...] = jnp.broadcast_to(own, square_ref.shape)
    store_message(out_ref, left, own)


VMEM = pl.BlockSpec(memory_space=pltpu.VMEM)
SMEM = pl.BlockSpec(memory_space=pltpu.SMEM)
LIMIT = pltpu.CompilerParams(vmem_limit_bytes=32 * 1024 * 1024)


def f32(*shape):
    return jax.ShapeDtypeStruct(shape, F32)


def message(n):
    return jax.ShapeDtypeStruct((n, MSG, CHANS), I16)


def apply_tiles(kernel, name, n_out, vec_tiles, sum_shape, meta, received, own, other):
    return pl.pallas_call(
        kernel,
        out_shape=message(n_out),
        in_specs=[SMEM, VMEM, VMEM, VMEM],
        out_specs=VMEM,
        scratch_shapes=[pltpu.VMEM((vec_tiles, TILE, 2 * CHANS), BF16), pltpu.VMEM(sum_shape, F32)],
        compiler_params=LIMIT,
        cost_estimate=pl.CostEstimate(
            flops=4 * 2 * SLOTS * TILE * TILE * CHANS, bytes_accessed=6 * 1024 * 1024, transcendentals=0
        ),
        name=name,
    )(meta, received, own, other)


def shards(rewards, tile_data, tile_slots, tile_count):
    core = lax.axis_index("core")
    swap = [(0, 1), (1, 0)]

    own = tile_data[0, 0]
    slots = jnp.concatenate([tile_slots[0, 0], tile_count[0, 0][None], jnp.zeros((3,), jnp.int32)])
    sent = lax.dynamic_slice_in_dim(rewards, (1 - core) * CHANS, CHANS, 1)
    kept = lax.dynamic_slice_in_dim(rewards, core * CHANS, CHANS, 1)
    arrived = lax.ppermute(sent, "core", swap)
    rewards_pair = jnp.where(
        core == 0, jnp.concatenate([kept, arrived], axis=0), jnp.concatenate([arrived, kept], axis=0)
    )
    other = lax.ppermute(own, "core", swap)
    other_slots = lax.ppermute(slots, "core", swap)
    meta = jnp.stack([slots, other_slots, jnp.full_like(slots, core)])

    def adjoint(received):
        out = apply_tiles(
            adjoint_kernel, "adjoint", N_ROWS, 4, (TILE_COLS, TILE, CHANS), meta, received, own, other
        )
        return lax.all_to_all(out, ROWS, 0, 0)

    def forward(received):
        out = apply_tiles(
            forward_kernel, "forward", N_COLS, TILE_COLS, (N_COLS, PAIR, CHANS), meta, received, own, other
        )
        return lax.all_to_all(out, COLS, 0, 0)

    def adjoint_end(received, left, right):
        first = right is None
        return pl.pallas_call(
            functools.partial(adjoint_end_kernel, first),
            out_shape=(f32(PAIR, CHANS), f32(PAIR, CHANS), f32(8, CHANS), message(N_ROWS)),
            in_specs=[VMEM] * (2 if first else 3),
            out_specs=(VMEM,) * 4,
            compiler_params=LIMIT,
            name="adjoint_end",
        )(received, left, *(() if first else (right,)))

    def forward_end(received, raw, unit):
        return pl.pallas_call(
            forward_end_kernel,
            out_shape=(f32(PAIR, CHANS), f32(PAIR, CHANS), f32(8, CHANS), f32(8, CHANS), message(N_COLS)),
            in_specs=[VMEM] * 3,
            out_specs=(VMEM,) * 5,
            compiler_params=LIMIT,
            name="forward_end",
        )(received, raw, unit)

    def sum_over_chips(square):
        spread = jnp.broadcast_to(square.reshape(1, 2, 128), (N_ROWS * N_COLS, 2, 128))
        return jnp.sum(lax.all_to_all(spread, ROWS + COLS, 0, 0), axis=0).reshape(CHANS)

    sends = pl.pallas_call(
        first_kernel, out_shape=message(N_COLS), in_specs=[VMEM], out_specs=VMEM, compiler_params=LIMIT, name="first"
    )(rewards_pair)
    raw, unit, beta_rows, sends = adjoint_end(adjoint(lax.all_to_all(sends, COLS, 0, 0)), rewards_pair, None)
    beta_first = beta_rows[0]
    estimate = jnp.zeros_like(rewards_pair)
    phibar = beta_first
    rhobar = None
    direction = None
    theta_rho = None
    sine_val = cosine = None
    for iteration in range(ITERS):
        received = forward(lax.all_to_all(sends, ROWS, 0, 0))
        left, right, alpha_rows, square_rows, sends = forward_end(received, raw, unit)
        alpha_val = alpha_rows[0]
        if iteration == 0:
            rhobar = alpha_val
            direction = right
        else:
            theta_val = sine_val * alpha_val
            rhobar = -cosine * alpha_val
            direction = right - theta_val / rho_val * direction
        if iteration < ITERS - 1:
            raw, unit, beta_rows, sends = adjoint_end(adjoint(lax.all_to_all(sends, COLS, 0, 0)), left, right)
            beta_val = beta_rows[0]
        else:
            beta_val = jnp.sqrt(sum_over_chips(square_rows[0]) + EPS)
            raw, unit, beta_rows, sends = adjoint_end(adjoint(lax.all_to_all(sends, COLS, 0, 0)), left, right)
        rho_val = jnp.sqrt(rhobar * rhobar + beta_val * beta_val)
        cosine = rhobar / rho_val
        sine_val = beta_val / rho_val
        phi_val = cosine * phibar
        phibar = sine_val * phibar
        estimate = estimate + phi_val / rho_val * direction
    residual = phibar / beta_first

    kept = lax.dynamic_slice_in_dim(estimate, core * STATES_DEV, STATES_DEV, 0)
    sent = lax.dynamic_slice_in_dim(estimate, (1 - core) * STATES_DEV, STATES_DEV, 0)
    arrived = lax.ppermute(sent, "core", swap)
    residual_other = lax.ppermute(residual, "core", swap)
    estimate_out = jnp.where(
        core == 0, jnp.concatenate([kept, arrived], axis=1), jnp.concatenate([arrived, kept], axis=1)
    )
    residual_out = jnp.where(
        core == 0, jnp.concatenate([residual, residual_other]), jnp.concatenate([residual_other, residual])
    )
    return (estimate_out, residual_out)


def solution(mesh):
    fine = Mesh(np.asarray(mesh.devices).reshape(SIZES), AXES)
    rows = ("z", "yh", "core")
    return jax.shard_map(
        shards,
        mesh=fine,
        in_specs=(
            P(AXES, None),
            P(rows, COLS, None, None, None),
            P(rows, COLS, None),
            P(rows, COLS),
        ),
        out_specs=(P(AXES, None), P()),
        check_vma=False,
    )
```

```python
import functools

import jax
import jax.numpy as jnp
import numpy as np
from jax import lax
from jax.experimental import pallas as pl
from jax.experimental.pallas import tpu as pltpu
from jax.sharding import Mesh, PartitionSpec as P

ITERS = 2
EPS = 1e-06
GAMMA = 0.9

AXES = ("z", "yh", "core", "x", "yl")
SIZES = (8, 2, 2, 4, 2)
ROWS = ("z", "yh")
COLS = ("x", "yl")
N_COLS = 8
TILE = 256
STATES_DEV = 64
PAIR = 2 * STATES_DEV
CORE_CHANS = 256
CHANS = 128
BLOCKS = 4
SLOTS = 12
FAR_FIRST = 4
TILE_COLS = 8
HEAD = 16
BITS = 14.0
BF16 = jnp.bfloat16
F32 = jnp.float32
I16 = jnp.int16


def to_i16(values):
    return values.astype(jnp.int32).astype(I16)


def scaled_exponent(largest):
    return jnp.ceil(jnp.log2(jnp.maximum(largest, 1e-30)))


def head_rows(exponent, square):
    square_exp = scaled_exponent(square)
    mantissa = square * jnp.exp2(-square_exp) * 16384.0
    high = jnp.round(mantissa)
    low = jnp.round((mantissa - high) * 16384.0)
    row = lax.broadcasted_iota(jnp.int32, (HEAD, exponent.shape[-1]), 0)
    rows = jnp.where(row == 0, exponent, jnp.where(row == 1, square_exp, jnp.where(row == 2, high, low)))
    return to_i16(rows)


def read_head(head):
    rows = head.astype(jnp.int32).astype(F32)
    step = jnp.exp2(rows[0:1] - BITS)
    square = (rows[2:3] + rows[3:4] * (1.0 / 16384.0)) * (1.0 / 16384.0) * jnp.exp2(rows[1:2])
    return step, square


def quantized(block):
    exponent = scaled_exponent(jnp.max(jnp.abs(block), axis=0, keepdims=True))
    return to_i16(jnp.round(block * jnp.exp2(BITS - exponent))), exponent


def store_message(out_ref, index, block, square):
    values, exponent = quantized(block)
    head = head_rows(exponent, square)
    rows = block.shape[0]
    for i in range(out_ref.shape[0]) if index is None else (index,):
        out_ref[i, :rows, :] = values
        out_ref[i, rows:, :] = head


def wide(values):
    return values.astype(jnp.int32).astype(F32)


def split_store(ref, index, rows, values):
    high = values.astype(BF16)
    chans = values.shape[-1]
    ref[index, rows, :chans] = high
    ref[index, rows, chans:] = (values - high.astype(F32)).astype(BF16)


def tile_at(refs, which, s):
    if which < 2:
        return refs[which][s]
    at = 2 * which - 2
    return refs[at][s] if s < FAR_FIRST else refs[at + 1][s - FAR_FIRST]


def column_of(meta_ref, which, s):
    return jnp.where(s < meta_ref[which, SLOTS], meta_ref[which, s] % TILE_COLS, TILE_COLS)


def forward_kernel(meta_ref, msg_ref, *refs):
    tile_refs, (out_ref, vec_ref, sum_ref) = refs[:-3], refs[-3:]
    square = jnp.zeros((1, CHANS), F32)
    for k in range(TILE_COLS):
        step, part = read_head(msg_ref[k, TILE:, :])
        square = square + part
        split_store(vec_ref, k, slice(None), wide(msg_ref[k, :TILE, :]) * step)
    vec_ref[TILE_COLS] = jnp.zeros((TILE, 2 * CHANS), BF16)
    for which in range(BLOCKS):
        block = meta_ref[BLOCKS, which]
        start = meta_ref[which, 0] // TILE_COLS
        for parity in range(2):
            slots = range(parity, SLOTS, 2)
            row = jnp.concatenate([tile_at(tile_refs, which, s) for s in slots], axis=1)
            vec = jnp.concatenate([vec_ref[column_of(meta_ref, which, s)] for s in slots], axis=0)
            total = jnp.dot(row, vec, preferred_element_type=F32)
            summed = total[:, :CHANS] + total[:, CHANS:]
            tile_row = (start + parity) % 2
            for q in range(4):
                sum_ref[tile_row * 4 + q, pl.ds(block * STATES_DEV, STATES_DEV), :] = summed[
                    q * STATES_DEV : (q + 1) * STATES_DEV
                ]
    for k in range(N_COLS):
        store_message(out_ref, k, sum_ref[k], square)


def adjoint_sums(meta_ref, msg_ref, tile_refs, vec_ref, sum_ref):
    chans = msg_ref.shape[-1]
    blocks = msg_ref.shape[1] // STATES_DEV
    square = jnp.zeros((1, chans), F32)
    for k in range(N_COLS):
        step, part = read_head(msg_ref[k, blocks * STATES_DEV :, :])
        square = square + part
        for block in range(blocks):
            values = wide(msg_ref[k, block * STATES_DEV : (block + 1) * STATES_DEV, :]) * step
            split_store(vec_ref, block * 2 + k // 4, pl.ds((k % 4) * STATES_DEV, STATES_DEV), values)
    sum_ref[...] = jnp.zeros_like(sum_ref)
    for which in range(blocks):
        block = meta_ref[BLOCKS, which] % blocks
        start = meta_ref[which, 0] // TILE_COLS
        for parity in range(2):
            vec = vec_ref[block * 2 + (start + parity) % 2]
            for s in range(parity, SLOTS, 2):
                product = lax.dot_general(
                    tile_at(tile_refs, which, s), vec, (((0,), (0,)), ((), ())), preferred_element_type=F32
                )
                sum_ref[column_of(meta_ref, which, s)] += product[:, :chans] + product[:, chans:]
    return square


def adjoint_kernel(meta_ref, msg_ref, *refs):
    tile_refs, (out_ref, vec_ref, sum_ref) = refs[:-3], refs[-3:]
    square = adjoint_sums(meta_ref, msg_ref, tile_refs, vec_ref, sum_ref)
    for k in range(TILE_COLS):
        store_message(out_ref, k, sum_ref[k], square)


def first_adjoint_kernel(meta_ref, msg_ref, *refs):
    tile_refs, (kept_ref, square_ref, out_ref, vec_ref, sum_ref) = refs[:-5], refs[-5:]
    square = adjoint_sums(meta_ref, msg_ref, tile_refs, vec_ref, sum_ref)
    square_ref[...] = jnp.broadcast_to(square[:, :CHANS], square_ref.shape)
    for k in range(TILE_COLS):
        kept_ref[k] = sum_ref[k, :, :CHANS]
        store_message(out_ref, k, sum_ref[k, :, CHANS:], square[:, CHANS:])


def combine_kernel(kept_ref, square_ref, msg_ref, out_ref):
    for k in range(TILE_COLS):
        step, square = read_head(msg_ref[k, TILE:, :])
        total = kept_ref[k] + wide(msg_ref[k, :TILE, :]) * step
        store_message(out_ref, k, total, square_ref[0:1] + square)


def summed_messages(msg_ref):
    total = jnp.zeros((TILE, CHANS), F32)
    square = jnp.zeros((1, CHANS), F32)
    for k in range(msg_ref.shape[0]):
        step, part = read_head(msg_ref[k, TILE:, :])
        total = total + wide(msg_ref[k, :TILE, :]) * step
        square = square + part
    return total, square


def first_kernel(rewards_ref, out_ref):
    rewards = rewards_ref[...]
    store_message(out_ref, None, rewards, jnp.sum(rewards * rewards, axis=0, keepdims=True))


def adjoint_end_kernel(first, msg_ref, left_ref, *refs):
    right_ref, (raw_ref, unit_ref, norm_ref, out_ref) = (None, refs) if first else (refs[0], refs[1:])
    total, square = summed_messages(msg_ref)
    beta = jnp.sqrt(square + EPS)
    unit = left_ref[...] / beta
    raw = unit - GAMMA * (total / beta)
    if not first:
        raw = raw - beta * right_ref[...]
    raw_ref[...] = raw
    unit_ref[...] = unit
    norm_ref[...] = jnp.broadcast_to(beta, norm_ref.shape)
    store_message(out_ref, None, raw, jnp.sum(raw * raw, axis=0, keepdims=True))


def forward_end_kernel(msg_ref, raw_ref, unit_ref, left_ref, right_ref, norm_ref, out_ref):
    total, square = summed_messages(msg_ref)
    alpha = jnp.sqrt(square + EPS)
    right = raw_ref[...] / alpha
    left = right - GAMMA * (total / alpha) - alpha * unit_ref[...]
    left_ref[...] = left
    right_ref[...] = right
    norm_ref[...] = jnp.broadcast_to(alpha, norm_ref.shape)
    store_message(out_ref, None, left, jnp.sum(left * left, axis=0, keepdims=True))


def last_end_kernel(msg_ref, raw_ref, unit_ref, out_ref):
    total, square = summed_messages(msg_ref)
    alpha = jnp.sqrt(square + EPS)
    left = raw_ref[...] / alpha - GAMMA * (total / alpha) - alpha * unit_ref[...]
    own = jnp.sum(left * left, axis=0, keepdims=True)
    out_ref[...] = jnp.broadcast_to(jnp.concatenate([own, alpha], axis=0)[None], out_ref.shape)


VMEM = pl.BlockSpec(memory_space=pltpu.VMEM)
SMEM = pl.BlockSpec(memory_space=pltpu.SMEM)
LIMIT = pltpu.CompilerParams(vmem_limit_bytes=32 * 1024 * 1024)


def f32(*shape):
    return jax.ShapeDtypeStruct(shape, F32)


def message(n, rows=TILE, chans=CHANS):
    return jax.ShapeDtypeStruct((n, rows + HEAD, chans), I16)


def apply_tiles(kernel, name, outs, vec_tiles, n_sums, chans, meta, received, tiles):
    return pl.pallas_call(
        kernel,
        out_shape=outs,
        in_specs=[SMEM] + [VMEM] * (1 + len(tiles)),
        out_specs=jax.tree.map(lambda _: VMEM, outs),
        scratch_shapes=[
            pltpu.VMEM((vec_tiles + 1, TILE, 2 * chans), BF16),
            pltpu.VMEM((n_sums + 1, TILE, chans), F32),
        ],
        compiler_params=LIMIT,
        cost_estimate=pl.CostEstimate(
            flops=4 * (BLOCKS * CHANS) * SLOTS * TILE * TILE, bytes_accessed=6 * 1024 * 1024, transcendentals=0
        ),
        name=name,
    )(meta, received, *tiles)


def shards(rewards, tile_data, tile_slots, tile_count):
    core, yh = lax.axis_index("core"), lax.axis_index("yh")
    swap = [(0, 1), (1, 0)]

    def in_order(at, kept, arrived, axis):
        return jnp.where(
            at == 0, jnp.concatenate([kept, arrived], axis=axis), jnp.concatenate([arrived, kept], axis=axis)
        )

    def exchange(name, at, values, axis):
        size = values.shape[axis] // 2
        kept = lax.dynamic_slice_in_dim(values, at * size, size, axis)
        return kept, lax.ppermute(lax.dynamic_slice_in_dim(values, (1 - at) * size, size, axis), name, swap)

    own = tile_data[0, 0]
    slots = jnp.concatenate([tile_slots[0, 0], tile_count[0, 0][None], jnp.zeros((3,), jnp.int32)])
    rewards_pair = in_order(core, *exchange("core", core, rewards, 1), 0)
    rewards_kept = lax.dynamic_slice_in_dim(rewards_pair, yh * CHANS, CHANS, 1)
    rewards_sent = lax.dynamic_slice_in_dim(rewards_pair, (1 - yh) * CHANS, CHANS, 1)
    rewards_arrived = lax.ppermute(rewards_sent, "yh", swap)
    pair = [own, lax.ppermute(own, "core", swap)]
    pair_slots = jnp.stack([slots, lax.ppermute(slots, "core", swap)])
    far_slots = lax.ppermute(pair_slots, "yh", swap)
    here, there = yh * 2, (1 - yh) * 2
    places = jnp.stack([here + core, here + 1 - core, there + core, there + 1 - core]).astype(jnp.int32)
    places = jnp.concatenate([places, jnp.zeros((12,), jnp.int32)])[None]

    def first_adjoint(received, own_last):
        pair_meta = jnp.concatenate([pair_slots, pair_slots, places])
        kept, square, sent = apply_tiles(
            first_adjoint_kernel,
            "first_adjoint",
            (f32(TILE_COLS, TILE, CHANS), f32(8, CHANS), message(TILE_COLS)),
            4, TILE_COLS, CORE_CHANS, pair_meta, received, pair,
        )
        arrived = lax.ppermute(sent, "yh", swap)
        own_last, *_ = lax.optimization_barrier((own_last, arrived, rewards_arrived, far_slots))
        far = lax.ppermute(own_last, "yh", swap)
        out = pl.pallas_call(
            combine_kernel,
            out_shape=message(TILE_COLS),
            in_specs=[VMEM] * 3,
            out_specs=VMEM,
            compiler_params=LIMIT,
            name="combine",
        )(kept, square, arrived)
        return out, far

    def adjoint(received):
        out = apply_tiles(
            adjoint_kernel, "adjoint", message(TILE_COLS), 8, TILE_COLS, CHANS, meta, received, tiles
        )
        return lax.all_to_all(out, "z", 0, 0)

    def forward(received):
        out = apply_tiles(forward_kernel, "forward", message(N_COLS), TILE_COLS, N_COLS, CHANS, meta, received, tiles)
        return lax.all_to_all(out, COLS, 0, 0)

    def adjoint_end(received, left, right):
        first = right is None
        return pl.pallas_call(
            functools.partial(adjoint_end_kernel, first),
            out_shape=(f32(TILE, CHANS), f32(TILE, CHANS), f32(8, CHANS), message(TILE_COLS)),
            in_specs=[VMEM] * (2 if first else 3),
            out_specs=(VMEM,) * 4,
            compiler_params=LIMIT,
            name="adjoint_end",
        )(received, left, *(() if first else (right,)))

    def forward_end(received, raw, unit):
        return pl.pallas_call(
            forward_end_kernel,
            out_shape=(f32(TILE, CHANS), f32(TILE, CHANS), f32(8, CHANS), message(N_COLS)),
            in_specs=[VMEM] * 3,
            out_specs=(VMEM,) * 4,
            compiler_params=LIMIT,
            name="forward_end",
        )(received, raw, unit)

    def last_end(received, raw, unit):
        spread = pl.pallas_call(
            last_end_kernel,
            out_shape=f32(128, 2, CHANS),
            in_specs=[VMEM] * 3,
            out_specs=VMEM,
            compiler_params=LIMIT,
            name="last_end",
        )(received, raw, unit)
        parts = lax.all_to_all(spread, ("yh", "z", "x", "yl"), 0, 0).reshape(2, 64, 2, CHANS)
        rows = jnp.stack([jnp.sum(parts[:, :, 0], axis=1), parts[:, 0, 1]]).reshape(2, CORE_CHANS)
        rows = in_order(core, rows, lax.ppermute(rows, "core", swap), 1)
        return rows[0], rows[1]

    def send_home(vectors, scalars):
        n = len(vectors)
        rows = jnp.stack(scalars)
        rows = jnp.concatenate([rows, jnp.zeros((8 - len(scalars), CHANS), F32)])
        size = PAIR
        stacked = jnp.stack(vectors)
        for name, at, last in (("yh", yh, False), ("core", core, True)):
            width = stacked.shape[-1]
            kept = lax.dynamic_slice_in_dim(stacked, at * size, size, 1).reshape(n * size, width)
            sent = lax.dynamic_slice_in_dim(stacked, (1 - at) * size, size, 1).reshape(n * size, width)
            arrived = lax.ppermute(jnp.concatenate([sent, rows]), name, swap)
            both = in_order(at, jnp.concatenate([kept, rows]), arrived, 1)
            stacked, rows = both[:-8].reshape(n, size, 2 * width), both[-8:]
            size //= 2
        return [stacked[i] for i in range(n)], [rows[i] for i in range(len(scalars))]

    sends = pl.pallas_call(
        first_kernel,
        out_shape=message(N_COLS, PAIR, CORE_CHANS),
        in_specs=[VMEM],
        out_specs=VMEM,
        compiler_params=LIMIT,
        name="first",
    )(jnp.concatenate([rewards_kept, rewards_sent], axis=1))
    own_first, _ = lax.optimization_barrier((own[:FAR_FIRST], sends))
    far_first = lax.ppermute(own_first, "yh", swap)
    received = lax.all_to_all(sends, COLS, 0, 0)
    meta = jnp.concatenate([pair_slots, far_slots, places])
    rewards_own = in_order(yh, rewards_kept, rewards_arrived, 0)
    sends, far_last = first_adjoint(received, own[FAR_FIRST:])
    raw, unit, beta_rows, sends = adjoint_end(lax.all_to_all(sends, "z", 0, 0), rewards_own, None)
    far_last, _ = lax.optimization_barrier((far_last, sends))
    far = [far_first, far_last]
    tiles = pair + far + [lax.ppermute(part, "core", swap) for part in far]
    raws, alphas, betas = [raw], [], [beta_rows[0]]
    for iteration in range(ITERS):
        received = forward(lax.all_to_all(sends, "z", 0, 0))
        if iteration == ITERS - 1:
            raws, scalars = send_home(raws, betas + alphas)
            next_square, last_alpha = last_end(received, raw, unit)
        left, right, alpha_rows, sends = forward_end(received, raw, unit)
        raw, unit, beta_rows, sends = adjoint_end(adjoint(lax.all_to_all(sends, COLS, 0, 0)), left, right)
        if iteration < ITERS - 1:
            raws.append(raw)
            alphas.append(alpha_rows[0])
            betas.append(beta_rows[0])
    betas, alphas = scalars[:ITERS] + [jnp.sqrt(next_square + EPS)], scalars[ITERS:] + [last_alpha]

    phibar, rhobar = betas[0], alphas[0]
    direction = [1.0 / alphas[0]]
    estimate = []
    for iteration in range(ITERS):
        beta_val = betas[iteration + 1]
        rho_val = jnp.sqrt(rhobar * rhobar + beta_val * beta_val)
        cosine = rhobar / rho_val
        sine_val = beta_val / rho_val
        phi_val = cosine * phibar
        phibar = sine_val * phibar
        weight = phi_val / rho_val
        estimate = [e + weight * d for e, d in zip(estimate + [0.0], direction)]
        if iteration < ITERS - 1:
            alpha_val = alphas[iteration + 1]
            theta_val = sine_val * alpha_val
            rhobar = -cosine * alpha_val
            direction = [-(theta_val / rho_val) * d for d in direction] + [1.0 / alpha_val]
    total = sum(e[None, :] * w for e, w in zip(estimate, raws))
    return (total, phibar / betas[0])


def solution(mesh):
    fine = Mesh(np.asarray(mesh.devices).reshape(SIZES), AXES)
    rows = ("z", "yh", "core")
    return jax.shard_map(
        shards,
        mesh=fine,
        in_specs=(
            P(AXES, None),
            P(rows, COLS, None, None, None),
            P(rows, COLS, None),
            P(rows, COLS),
        ),
        out_specs=(P(AXES, None), P()),
        check_vma=False,
    )
```

```python
import functools

import jax
import jax.numpy as jnp
import numpy as np
from jax import lax
from jax.experimental import pallas as pl
from jax.experimental.pallas import tpu as pltpu
from jax.sharding import Mesh, PartitionSpec as P

ITERS = 2
EPS = 1e-06
GAMMA = 0.9

AXES = ("z", "yh", "core", "x", "yl")
SIZES = (8, 2, 2, 4, 2)
ROWS = ("z", "yh")
COLS = ("x", "yl")
N_COLS = 8
TILE = 256
STATES_DEV = 64
PAIR = 2 * STATES_DEV
CORE_CHANS = 256
CHANS = 128
BLOCKS = 4
SLOTS = 12
PART = 6
TILE_COLS = 8
HEAD = 16
BITS = 14.0
BF16 = jnp.bfloat16
F32 = jnp.float32
I16 = jnp.int16


def to_i16(values):
    return values.astype(jnp.int32).astype(I16)


def scaled_exponent(largest):
    return jnp.ceil(jnp.log2(jnp.maximum(largest, 1e-30)))


def head_rows(exponent, square):
    square_exp = scaled_exponent(square)
    mantissa = square * jnp.exp2(-square_exp) * 16384.0
    high = jnp.round(mantissa)
    low = jnp.round((mantissa - high) * 16384.0)
    row = lax.broadcasted_iota(jnp.int32, (HEAD, exponent.shape[-1]), 0)
    rows = jnp.where(row == 0, exponent, jnp.where(row == 1, square_exp, jnp.where(row == 2, high, low)))
    return to_i16(rows)


def read_head(head):
    rows = head.astype(jnp.int32).astype(F32)
    step = jnp.exp2(rows[0:1] - BITS)
    square = (rows[2:3] + rows[3:4] * (1.0 / 16384.0)) * (1.0 / 16384.0) * jnp.exp2(rows[1:2])
    return step, square


def quantized(block):
    exponent = scaled_exponent(jnp.max(jnp.abs(block), axis=0, keepdims=True))
    return to_i16(jnp.round(block * jnp.exp2(BITS - exponent))), exponent


def store_message(out_ref, index, block, square):
    values, exponent = quantized(block)
    head = head_rows(exponent, square)
    rows = block.shape[0]
    for i in range(out_ref.shape[0]) if index is None else (index,):
        out_ref[i, :rows, :] = values
        out_ref[i, rows:, :] = head


def wide(values):
    return values.astype(jnp.int32).astype(F32)


def split_store(ref, index, rows, values):
    high = values.astype(BF16)
    chans = values.shape[-1]
    ref[index, rows, :chans] = high
    ref[index, rows, chans:] = (values - high.astype(F32)).astype(BF16)


def tile_at(refs, which, s):
    return refs[which][s] if which < 3 else refs[3 + s // PART][s % PART]


def column_of(meta_ref, which, s):
    return jnp.where(s < meta_ref[which, SLOTS], meta_ref[which, s] % TILE_COLS, TILE_COLS)


def forward_kernel(meta_ref, msg_ref, *refs):
    tile_refs, (out_ref, vec_ref, sum_ref) = refs[:-3], refs[-3:]
    square = jnp.zeros((1, CHANS), F32)
    for k in range(TILE_COLS):
        step, part = read_head(msg_ref[k, TILE:, :])
        square = square + part
        split_store(vec_ref, k, slice(None), wide(msg_ref[k, :TILE, :]) * step)
    vec_ref[TILE_COLS] = jnp.zeros((TILE, 2 * CHANS), BF16)
    for which in range(BLOCKS):
        block = meta_ref[BLOCKS, which]
        start = meta_ref[which, 0] // TILE_COLS
        for parity in range(2):
            slots = range(parity, SLOTS, 2)
            row = jnp.concatenate([tile_at(tile_refs, which, s) for s in slots], axis=1)
            vec = jnp.concatenate([vec_ref[column_of(meta_ref, which, s)] for s in slots], axis=0)
            total = jnp.dot(row, vec, preferred_element_type=F32)
            summed = total[:, :CHANS] + total[:, CHANS:]
            tile_row = (start + parity) % 2
            for q in range(4):
                sum_ref[tile_row * 4 + q, pl.ds(block * STATES_DEV, STATES_DEV), :] = summed[
                    q * STATES_DEV : (q + 1) * STATES_DEV
                ]
    for k in range(N_COLS):
        store_message(out_ref, k, sum_ref[k], square)


def adjoint_sums(meta_ref, msg_ref, tile_refs, vec_ref, sum_ref):
    chans = msg_ref.shape[-1]
    blocks = msg_ref.shape[1] // STATES_DEV
    square = jnp.zeros((1, chans), F32)
    for k in range(N_COLS):
        step, part = read_head(msg_ref[k, blocks * STATES_DEV :, :])
        square = square + part
        for block in range(blocks):
            values = wide(msg_ref[k, block * STATES_DEV : (block + 1) * STATES_DEV, :]) * step
            split_store(vec_ref, block * 2 + k // 4, pl.ds((k % 4) * STATES_DEV, STATES_DEV), values)
    sum_ref[...] = jnp.zeros_like(sum_ref)
    for which in range(blocks):
        block = meta_ref[BLOCKS, which] % blocks
        start = meta_ref[which, 0] // TILE_COLS
        for parity in range(2):
            vec = vec_ref[block * 2 + (start + parity) % 2]
            for s in range(parity, SLOTS, 2):
                product = lax.dot_general(
                    tile_at(tile_refs, which, s), vec, (((0,), (0,)), ((), ())), preferred_element_type=F32
                )
                sum_ref[column_of(meta_ref, which, s)] += product[:, :chans] + product[:, chans:]
    return square


def adjoint_kernel(meta_ref, msg_ref, *refs):
    tile_refs, (out_ref, vec_ref, sum_ref) = refs[:-3], refs[-3:]
    square = adjoint_sums(meta_ref, msg_ref, tile_refs, vec_ref, sum_ref)
    for k in range(TILE_COLS):
        store_message(out_ref, k, sum_ref[k], square)


def first_adjoint_kernel(meta_ref, msg_ref, *refs):
    tile_refs, (kept_ref, square_ref, out_ref, vec_ref, sum_ref) = refs[:-5], refs[-5:]
    square = adjoint_sums(meta_ref, msg_ref, tile_refs, vec_ref, sum_ref)
    square_ref[...] = jnp.broadcast_to(square[:, :CHANS], square_ref.shape)
    for k in range(TILE_COLS):
        kept_ref[k] = sum_ref[k, :, :CHANS]
        store_message(out_ref, k, sum_ref[k, :, CHANS:], square[:, CHANS:])


def combine_kernel(kept_ref, square_ref, msg_ref, out_ref):
    for k in range(TILE_COLS):
        step, square = read_head(msg_ref[k, TILE:, :])
        total = kept_ref[k] + wide(msg_ref[k, :TILE, :]) * step
        store_message(out_ref, k, total, square_ref[0:1] + square)


def summed_messages(msg_ref):
    total = jnp.zeros((TILE, CHANS), F32)
    square = jnp.zeros((1, CHANS), F32)
    for k in range(msg_ref.shape[0]):
        step, part = read_head(msg_ref[k, TILE:, :])
        total = total + wide(msg_ref[k, :TILE, :]) * step
        square = square + part
    return total, square


def first_kernel(rewards_ref, out_ref):
    rewards = rewards_ref[...]
    store_message(out_ref, None, rewards, jnp.sum(rewards * rewards, axis=0, keepdims=True))


def adjoint_end_kernel(first, msg_ref, left_ref, *refs):
    right_ref, (raw_ref, unit_ref, norm_ref, out_ref) = (None, refs) if first else (refs[0], refs[1:])
    total, square = summed_messages(msg_ref)
    beta = jnp.sqrt(square + EPS)
    unit = left_ref[...] / beta
    raw = unit - GAMMA * (total / beta)
    if not first:
        raw = raw - beta * right_ref[...]
    raw_ref[...] = raw
    unit_ref[...] = unit
    norm_ref[...] = jnp.broadcast_to(beta, norm_ref.shape)
    store_message(out_ref, None, raw, jnp.sum(raw * raw, axis=0, keepdims=True))


def forward_end_kernel(msg_ref, raw_ref, unit_ref, left_ref, right_ref, norm_ref, out_ref):
    total, square = summed_messages(msg_ref)
    alpha = jnp.sqrt(square + EPS)
    right = raw_ref[...] / alpha
    left = right - GAMMA * (total / alpha) - alpha * unit_ref[...]
    left_ref[...] = left
    right_ref[...] = right
    norm_ref[...] = jnp.broadcast_to(alpha, norm_ref.shape)
    store_message(out_ref, None, left, jnp.sum(left * left, axis=0, keepdims=True))


def last_end_kernel(msg_ref, raw_ref, unit_ref, out_ref):
    total, square = summed_messages(msg_ref)
    alpha = jnp.sqrt(square + EPS)
    left = raw_ref[...] / alpha - GAMMA * (total / alpha) - alpha * unit_ref[...]
    own = jnp.sum(left * left, axis=0, keepdims=True)
    out_ref[...] = jnp.broadcast_to(jnp.concatenate([own, alpha], axis=0)[None], out_ref.shape)


VMEM = pl.BlockSpec(memory_space=pltpu.VMEM)
SMEM = pl.BlockSpec(memory_space=pltpu.SMEM)
LIMIT = pltpu.CompilerParams(vmem_limit_bytes=32 * 1024 * 1024)


def f32(*shape):
    return jax.ShapeDtypeStruct(shape, F32)


def message(n, rows=TILE, chans=CHANS):
    return jax.ShapeDtypeStruct((n, rows + HEAD, chans), I16)


def apply_tiles(kernel, name, outs, vec_tiles, n_sums, chans, meta, received, tiles):
    return pl.pallas_call(
        kernel,
        out_shape=outs,
        in_specs=[SMEM] + [VMEM] * (1 + len(tiles)),
        out_specs=jax.tree.map(lambda _: VMEM, outs),
        scratch_shapes=[
            pltpu.VMEM((vec_tiles + 1, TILE, 2 * chans), BF16),
            pltpu.VMEM((n_sums + 1, TILE, chans), F32),
        ],
        compiler_params=LIMIT,
        cost_estimate=pl.CostEstimate(
            flops=4 * (BLOCKS * CHANS) * SLOTS * TILE * TILE, bytes_accessed=6 * 1024 * 1024, transcendentals=0
        ),
        name=name,
    )(meta, received, *tiles)


def shards(rewards, tile_data, tile_slots, tile_count):
    core, yh = lax.axis_index("core"), lax.axis_index("yh")
    swap = [(0, 1), (1, 0)]

    def in_order(at, kept, arrived, axis):
        return jnp.where(
            at == 0, jnp.concatenate([kept, arrived], axis=axis), jnp.concatenate([arrived, kept], axis=axis)
        )

    def exchange(name, at, values, axis):
        size = values.shape[axis] // 2
        kept = lax.dynamic_slice_in_dim(values, at * size, size, axis)
        return kept, lax.ppermute(lax.dynamic_slice_in_dim(values, (1 - at) * size, size, axis), name, swap)

    own = tile_data[0, 0]
    slots = jnp.concatenate([tile_slots[0, 0], tile_count[0, 0][None], jnp.zeros((3,), jnp.int32)])
    rewards_pair = in_order(core, *exchange("core", core, rewards, 1), 0)
    rewards_kept = lax.dynamic_slice_in_dim(rewards_pair, yh * CHANS, CHANS, 1)
    rewards_sent = lax.dynamic_slice_in_dim(rewards_pair, (1 - yh) * CHANS, CHANS, 1)
    rewards_arrived = lax.ppermute(rewards_sent, "yh", swap)
    pair = [own, lax.ppermute(own, "core", swap)]
    pair_slots = jnp.stack([slots, lax.ppermute(slots, "core", swap)])
    far_slots = lax.ppermute(pair_slots, "yh", swap)
    here, there = yh * 2, (1 - yh) * 2
    places = jnp.stack([here + core, here + 1 - core, there + core, there + 1 - core]).astype(jnp.int32)
    places = jnp.concatenate([places, jnp.zeros((12,), jnp.int32)])[None]

    def first_adjoint(received, own):
        pair_meta = jnp.concatenate([pair_slots, pair_slots, places])
        kept, square, sent = apply_tiles(
            first_adjoint_kernel,
            "first_adjoint",
            (f32(TILE_COLS, TILE, CHANS), f32(8, CHANS), message(TILE_COLS)),
            4, TILE_COLS, CORE_CHANS, pair_meta, received, pair,
        )
        arrived = lax.ppermute(sent, "yh", swap)
        own, *_ = lax.optimization_barrier((own, arrived, rewards_arrived, far_slots))
        far = lax.ppermute(own, "yh", swap)
        out = pl.pallas_call(
            combine_kernel,
            out_shape=message(TILE_COLS),
            in_specs=[VMEM] * 3,
            out_specs=VMEM,
            compiler_params=LIMIT,
            name="combine",
        )(kept, square, arrived)
        return out, far

    def adjoint(received):
        out = apply_tiles(
            adjoint_kernel, "adjoint", message(TILE_COLS), 8, TILE_COLS, CHANS, meta, received, tiles
        )
        return lax.all_to_all(out, "z", 0, 0)

    def forward(received):
        out = apply_tiles(forward_kernel, "forward", message(N_COLS), TILE_COLS, N_COLS, CHANS, meta, received, tiles)
        return lax.all_to_all(out, COLS, 0, 0)

    def adjoint_end(received, left, right):
        first = right is None
        return pl.pallas_call(
            functools.partial(adjoint_end_kernel, first),
            out_shape=(f32(TILE, CHANS), f32(TILE, CHANS), f32(8, CHANS), message(TILE_COLS)),
            in_specs=[VMEM] * (2 if first else 3),
            out_specs=(VMEM,) * 4,
            compiler_params=LIMIT,
            name="adjoint_end",
        )(received, left, *(() if first else (right,)))

    def forward_end(received, raw, unit):
        return pl.pallas_call(
            forward_end_kernel,
            out_shape=(f32(TILE, CHANS), f32(TILE, CHANS), f32(8, CHANS), message(N_COLS)),
            in_specs=[VMEM] * 3,
            out_specs=(VMEM,) * 4,
            compiler_params=LIMIT,
            name="forward_end",
        )(received, raw, unit)

    def last_end(received, raw, unit):
        spread = pl.pallas_call(
            last_end_kernel,
            out_shape=f32(128, 2, CHANS),
            in_specs=[VMEM] * 3,
            out_specs=VMEM,
            compiler_params=LIMIT,
            name="last_end",
        )(received, raw, unit)
        parts = lax.all_to_all(spread, ("yh", "z", "x", "yl"), 0, 0).reshape(2, 64, 2, CHANS)
        rows = jnp.stack([jnp.sum(parts[:, :, 0], axis=1), parts[:, 0, 1]]).reshape(2, CORE_CHANS)
        rows = in_order(core, rows, lax.ppermute(rows, "core", swap), 1)
        return rows[0], rows[1]

    def send_home(vectors, scalars):
        n = len(vectors)
        rows = jnp.stack(scalars)
        rows = jnp.concatenate([rows, jnp.zeros((8 - len(scalars), CHANS), F32)])
        size = PAIR
        stacked = jnp.stack(vectors)
        for name, at, last in (("yh", yh, False), ("core", core, True)):
            width = stacked.shape[-1]
            kept = lax.dynamic_slice_in_dim(stacked, at * size, size, 1).reshape(n * size, width)
            sent = lax.dynamic_slice_in_dim(stacked, (1 - at) * size, size, 1).reshape(n * size, width)
            arrived = lax.ppermute(jnp.concatenate([sent, rows]), name, swap)
            both = in_order(at, jnp.concatenate([kept, rows]), arrived, 1)
            stacked, rows = both[:-8].reshape(n, size, 2 * width), both[-8:]
            size //= 2
        return [stacked[i] for i in range(n)], [rows[i] for i in range(len(scalars))]

    sends = pl.pallas_call(
        first_kernel,
        out_shape=message(N_COLS, PAIR, CORE_CHANS),
        in_specs=[VMEM],
        out_specs=VMEM,
        compiler_params=LIMIT,
        name="first",
    )(jnp.concatenate([rewards_kept, rewards_sent], axis=1))
    received = lax.all_to_all(sends, COLS, 0, 0)
    meta = jnp.concatenate([pair_slots, far_slots, places])
    rewards_own = in_order(yh, rewards_kept, rewards_arrived, 0)
    sends, far = first_adjoint(received, own)
    raw, unit, beta_rows, sends = adjoint_end(lax.all_to_all(sends, "z", 0, 0), rewards_own, None)
    far, _ = lax.optimization_barrier((far, sends))
    tiles = pair + [far] + [lax.ppermute(part, "core", swap) for part in (far[:PART], far[PART:])]
    raws, alphas, betas = [raw], [], [beta_rows[0]]
    for iteration in range(ITERS):
        received = forward(lax.all_to_all(sends, "z", 0, 0))
        if iteration == ITERS - 1:
            raws, scalars = send_home(raws, betas + alphas)
            next_square, last_alpha = last_end(received, raw, unit)
        left, right, alpha_rows, sends = forward_end(received, raw, unit)
        raw, unit, beta_rows, sends = adjoint_end(adjoint(lax.all_to_all(sends, COLS, 0, 0)), left, right)
        if iteration < ITERS - 1:
            raws.append(raw)
            alphas.append(alpha_rows[0])
            betas.append(beta_rows[0])
    betas, alphas = scalars[:ITERS] + [jnp.sqrt(next_square + EPS)], scalars[ITERS:] + [last_alpha]

    phibar, rhobar = betas[0], alphas[0]
    direction = [1.0 / alphas[0]]
    estimate = []
    for iteration in range(ITERS):
        beta_val = betas[iteration + 1]
        rho_val = jnp.sqrt(rhobar * rhobar + beta_val * beta_val)
        cosine = rhobar / rho_val
        sine_val = beta_val / rho_val
        phi_val = cosine * phibar
        phibar = sine_val * phibar
        weight = phi_val / rho_val
        estimate = [e + weight * d for e, d in zip(estimate + [0.0], direction)]
        if iteration < ITERS - 1:
            alpha_val = alphas[iteration + 1]
            theta_val = sine_val * alpha_val
            rhobar = -cosine * alpha_val
            direction = [-(theta_val / rho_val) * d for d in direction] + [1.0 / alpha_val]
    total = sum(e[None, :] * w for e, w in zip(estimate, raws))
    return (total, phibar / betas[0])


def solution(mesh):
    fine = Mesh(np.asarray(mesh.devices).reshape(SIZES), AXES)
    rows = ("z", "yh", "core")
    return jax.shard_map(
        shards,
        mesh=fine,
        in_specs=(
            P(AXES, None),
            P(rows, COLS, None, None, None),
            P(rows, COLS, None),
            P(rows, COLS),
        ),
        out_specs=(P(AXES, None), P()),
        check_vma=False,
    )
```

```python
import functools

import jax
import jax.numpy as jnp
import numpy as np
from jax import lax
from jax.experimental import pallas as pl
from jax.experimental.pallas import tpu as pltpu
from jax.sharding import Mesh, PartitionSpec as P

ITERS = 2
EPS = 1e-06
GAMMA = 0.9

AXES = ("z", "yh", "core", "x", "yl")
SIZES = (8, 2, 2, 4, 2)
ROWS = ("z", "yh")
COLS = ("x", "yl")
N_COLS = 8
TILE = 256
STATES_DEV = 64
PAIR = 2 * STATES_DEV
CORE_CHANS = 256
CHANS = 128
BLOCKS = 4
SLOTS = 12
PART = 6
TILE_COLS = 8
HEAD = 16
BITS = 14.0
BF16 = jnp.bfloat16
F32 = jnp.float32
I16 = jnp.int16


def to_i16(values):
    return values.astype(jnp.int32).astype(I16)


def scaled_exponent(largest):
    return jnp.ceil(jnp.log2(jnp.maximum(largest, 1e-30)))


def head_rows(exponent, square):
    square_exp = scaled_exponent(square)
    mantissa = square * jnp.exp2(-square_exp) * 16384.0
    high = jnp.round(mantissa)
    low = jnp.round((mantissa - high) * 16384.0)
    row = lax.broadcasted_iota(jnp.int32, (HEAD, exponent.shape[-1]), 0)
    rows = jnp.where(row == 0, exponent, jnp.where(row == 1, square_exp, jnp.where(row == 2, high, low)))
    return to_i16(rows)


def read_head(head):
    rows = head.astype(jnp.int32).astype(F32)
    step = jnp.exp2(rows[0:1] - BITS)
    square = (rows[2:3] + rows[3:4] * (1.0 / 16384.0)) * (1.0 / 16384.0) * jnp.exp2(rows[1:2])
    return step, square


def quantized(block):
    exponent = scaled_exponent(jnp.max(jnp.abs(block), axis=0, keepdims=True))
    return to_i16(jnp.round(block * jnp.exp2(BITS - exponent))), exponent


def store_message(out_ref, index, block, square):
    values, exponent = quantized(block)
    head = head_rows(exponent, square)
    rows = block.shape[0]
    for i in range(out_ref.shape[0]) if index is None else (index,):
        out_ref[i, :rows, :] = values
        out_ref[i, rows:, :] = head


def wide(values):
    return values.astype(jnp.int32).astype(F32)


def split_store(ref, index, rows, values):
    high = values.astype(BF16)
    chans = values.shape[-1]
    ref[index, rows, :chans] = high
    ref[index, rows, chans:] = (values - high.astype(F32)).astype(BF16)


def tile_at(refs, which, s):
    return refs[which][s] if which < 3 else refs[3 + s // PART][s % PART]


def column_of(meta_ref, which, s):
    return jnp.where(s < meta_ref[which, SLOTS], meta_ref[which, s] % TILE_COLS, TILE_COLS)


def forward_kernel(meta_ref, msg_ref, *refs):
    tile_refs, (out_ref, vec_ref, sum_ref) = refs[:-3], refs[-3:]
    square = jnp.zeros((1, CHANS), F32)
    for k in range(TILE_COLS):
        step, part = read_head(msg_ref[k, TILE:, :])
        square = square + part
        split_store(vec_ref, k, slice(None), wide(msg_ref[k, :TILE, :]) * step)
    vec_ref[TILE_COLS] = jnp.zeros((TILE, 2 * CHANS), BF16)
    for which in range(BLOCKS):
        block = meta_ref[BLOCKS, which]
        start = meta_ref[which, 0] // TILE_COLS
        for parity in range(2):
            slots = range(parity, SLOTS, 2)
            row = jnp.concatenate([tile_at(tile_refs, which, s) for s in slots], axis=1)
            vec = jnp.concatenate([vec_ref[column_of(meta_ref, which, s)] for s in slots], axis=0)
            total = jnp.dot(row, vec, preferred_element_type=F32)
            summed = total[:, :CHANS] + total[:, CHANS:]
            tile_row = (start + parity) % 2
            for q in range(4):
                sum_ref[tile_row * 4 + q, pl.ds(block * STATES_DEV, STATES_DEV), :] = summed[
                    q * STATES_DEV : (q + 1) * STATES_DEV
                ]
    for k in range(N_COLS):
        store_message(out_ref, k, sum_ref[k], square)


def adjoint_sums(meta_ref, msg_ref, tile_refs, vec_ref, sum_ref, first=0):
    chans = sum_ref.shape[-1]
    lanes = slice(first, first + chans)
    blocks = msg_ref.shape[1] // STATES_DEV
    square = jnp.zeros((1, chans), F32)
    for k in range(N_COLS):
        step, part = read_head(msg_ref[k, blocks * STATES_DEV :, lanes])
        square = square + part
        for block in range(blocks):
            values = wide(msg_ref[k, block * STATES_DEV : (block + 1) * STATES_DEV, lanes]) * step
            split_store(vec_ref, block * 2 + k // 4, pl.ds((k % 4) * STATES_DEV, STATES_DEV), values)
    sum_ref[...] = jnp.zeros_like(sum_ref)
    for which in range(blocks):
        block = meta_ref[BLOCKS, which] % blocks
        start = meta_ref[which, 0] // TILE_COLS
        for parity in range(2):
            vec = vec_ref[block * 2 + (start + parity) % 2]
            for s in range(parity, SLOTS, 2):
                product = lax.dot_general(
                    tile_at(tile_refs, which, s), vec, (((0,), (0,)), ((), ())), preferred_element_type=F32
                )
                sum_ref[column_of(meta_ref, which, s)] += product[:, :chans] + product[:, chans:]
    return square


def adjoint_kernel(meta_ref, msg_ref, *refs):
    tile_refs, (out_ref, vec_ref, sum_ref) = refs[:-3], refs[-3:]
    square = adjoint_sums(meta_ref, msg_ref, tile_refs, vec_ref, sum_ref)
    for k in range(TILE_COLS):
        store_message(out_ref, k, sum_ref[k], square)


def sent_adjoint_kernel(meta_ref, msg_ref, *refs):
    tile_refs, (out_ref, vec_ref, sum_ref) = refs[:-3], refs[-3:]
    square = adjoint_sums(meta_ref, msg_ref, tile_refs, vec_ref, sum_ref, CHANS)
    for k in range(TILE_COLS):
        store_message(out_ref, k, sum_ref[k], square)


def kept_adjoint_kernel(meta_ref, msg_ref, *refs):
    tile_refs, (kept_ref, square_ref, vec_ref, sum_ref) = refs[:-4], refs[-4:]
    square = adjoint_sums(meta_ref, msg_ref, tile_refs, vec_ref, sum_ref)
    square_ref[...] = jnp.broadcast_to(square, square_ref.shape)
    for k in range(TILE_COLS):
        kept_ref[k] = sum_ref[k]


def combine_kernel(kept_ref, square_ref, msg_ref, out_ref):
    for k in range(TILE_COLS):
        step, square = read_head(msg_ref[k, TILE:, :])
        total = kept_ref[k] + wide(msg_ref[k, :TILE, :]) * step
        store_message(out_ref, k, total, square_ref[0:1] + square)


def summed_messages(msg_ref):
    total = jnp.zeros((TILE, CHANS), F32)
    square = jnp.zeros((1, CHANS), F32)
    for k in range(msg_ref.shape[0]):
        step, part = read_head(msg_ref[k, TILE:, :])
        total = total + wide(msg_ref[k, :TILE, :]) * step
        square = square + part
    return total, square


def first_kernel(rewards_ref, out_ref):
    rewards = rewards_ref[...]
    store_message(out_ref, None, rewards, jnp.sum(rewards * rewards, axis=0, keepdims=True))


def adjoint_end_kernel(first, msg_ref, left_ref, *refs):
    right_ref, (raw_ref, unit_ref, norm_ref, out_ref) = (None, refs) if first else (refs[0], refs[1:])
    total, square = summed_messages(msg_ref)
    beta = jnp.sqrt(square + EPS)
    unit = left_ref[...] / beta
    raw = unit - GAMMA * (total / beta)
    if not first:
        raw = raw - beta * right_ref[...]
    raw_ref[...] = raw
    unit_ref[...] = unit
    norm_ref[...] = jnp.broadcast_to(beta, norm_ref.shape)
    store_message(out_ref, None, raw, jnp.sum(raw * raw, axis=0, keepdims=True))


def forward_end_kernel(msg_ref, raw_ref, unit_ref, left_ref, right_ref, norm_ref, out_ref):
    total, square = summed_messages(msg_ref)
    alpha = jnp.sqrt(square + EPS)
    right = raw_ref[...] / alpha
    left = right - GAMMA * (total / alpha) - alpha * unit_ref[...]
    left_ref[...] = left
    right_ref[...] = right
    norm_ref[...] = jnp.broadcast_to(alpha, norm_ref.shape)
    store_message(out_ref, None, left, jnp.sum(left * left, axis=0, keepdims=True))


def last_end_kernel(msg_ref, raw_ref, unit_ref, out_ref):
    total, square = summed_messages(msg_ref)
    alpha = jnp.sqrt(square + EPS)
    left = raw_ref[...] / alpha - GAMMA * (total / alpha) - alpha * unit_ref[...]
    own = jnp.sum(left * left, axis=0, keepdims=True)
    out_ref[...] = jnp.broadcast_to(jnp.concatenate([own, alpha], axis=0)[None], out_ref.shape)


VMEM = pl.BlockSpec(memory_space=pltpu.VMEM)
SMEM = pl.BlockSpec(memory_space=pltpu.SMEM)
LIMIT = pltpu.CompilerParams(vmem_limit_bytes=32 * 1024 * 1024)


def f32(*shape):
    return jax.ShapeDtypeStruct(shape, F32)


def message(n, rows=TILE, chans=CHANS):
    return jax.ShapeDtypeStruct((n, rows + HEAD, chans), I16)


def apply_tiles(kernel, name, outs, vec_tiles, n_sums, chans, meta, received, tiles):
    return pl.pallas_call(
        kernel,
        out_shape=outs,
        in_specs=[SMEM] + [VMEM] * (1 + len(tiles)),
        out_specs=jax.tree.map(lambda _: VMEM, outs),
        scratch_shapes=[
            pltpu.VMEM((vec_tiles + 1, TILE, 2 * chans), BF16),
            pltpu.VMEM((n_sums + 1, TILE, chans), F32),
        ],
        compiler_params=LIMIT,
        cost_estimate=pl.CostEstimate(
            flops=4 * (BLOCKS * CHANS) * SLOTS * TILE * TILE, bytes_accessed=6 * 1024 * 1024, transcendentals=0
        ),
        name=name,
    )(meta, received, *tiles)


def shards(rewards, tile_data, tile_slots, tile_count):
    core, yh = lax.axis_index("core"), lax.axis_index("yh")
    swap = [(0, 1), (1, 0)]

    def in_order(at, kept, arrived, axis):
        return jnp.where(
            at == 0, jnp.concatenate([kept, arrived], axis=axis), jnp.concatenate([arrived, kept], axis=axis)
        )

    def exchange(name, at, values, axis):
        size = values.shape[axis] // 2
        kept = lax.dynamic_slice_in_dim(values, at * size, size, axis)
        return kept, lax.ppermute(lax.dynamic_slice_in_dim(values, (1 - at) * size, size, axis), name, swap)

    own = tile_data[0, 0]
    slots = jnp.concatenate([tile_slots[0, 0], tile_count[0, 0][None], jnp.zeros((3,), jnp.int32)])
    rewards_pair = in_order(core, *exchange("core", core, rewards, 1), 0)
    rewards_kept = lax.dynamic_slice_in_dim(rewards_pair, yh * CHANS, CHANS, 1)
    rewards_sent = lax.dynamic_slice_in_dim(rewards_pair, (1 - yh) * CHANS, CHANS, 1)
    rewards_arrived = lax.ppermute(rewards_sent, "yh", swap)
    pair = [own, lax.ppermute(own, "core", swap)]
    pair_slots = jnp.stack([slots, lax.ppermute(slots, "core", swap)])
    far_slots = lax.ppermute(pair_slots, "yh", swap)
    here, there = yh * 2, (1 - yh) * 2
    places = jnp.stack([here + core, here + 1 - core, there + core, there + 1 - core]).astype(jnp.int32)
    places = jnp.concatenate([places, jnp.zeros((12,), jnp.int32)])[None]

    def first_adjoint(received, own):
        pair_meta = jnp.concatenate([pair_slots, pair_slots, places])
        sent = apply_tiles(
            sent_adjoint_kernel, "sent_adjoint", message(TILE_COLS), 4, TILE_COLS, CHANS, pair_meta, received, pair
        )
        received, sent = lax.optimization_barrier((received, sent))
        kept, square = apply_tiles(
            kept_adjoint_kernel,
            "kept_adjoint",
            (f32(TILE_COLS, TILE, CHANS), f32(8, CHANS)),
            4, TILE_COLS, CHANS, pair_meta, received, pair,
        )
        arrived = lax.ppermute(sent, "yh", swap)
        own, *_ = lax.optimization_barrier((own, arrived, kept))
        far = lax.ppermute(own, "yh", swap)
        out = pl.pallas_call(
            combine_kernel,
            out_shape=message(TILE_COLS),
            in_specs=[VMEM] * 3,
            out_specs=VMEM,
            compiler_params=LIMIT,
            name="combine",
        )(kept, square, arrived)
        return out, far

    def adjoint(received):
        out = apply_tiles(
            adjoint_kernel, "adjoint", message(TILE_COLS), 8, TILE_COLS, CHANS, meta, received, tiles
        )
        return lax.all_to_all(out, "z", 0, 0)

    def forward(received):
        out = apply_tiles(forward_kernel, "forward", message(N_COLS), TILE_COLS, N_COLS, CHANS, meta, received, tiles)
        return lax.all_to_all(out, COLS, 0, 0)

    def adjoint_end(received, left, right):
        first = right is None
        return pl.pallas_call(
            functools.partial(adjoint_end_kernel, first),
            out_shape=(f32(TILE, CHANS), f32(TILE, CHANS), f32(8, CHANS), message(TILE_COLS)),
            in_specs=[VMEM] * (2 if first else 3),
            out_specs=(VMEM,) * 4,
            compiler_params=LIMIT,
            name="adjoint_end",
        )(received, left, *(() if first else (right,)))

    def forward_end(received, raw, unit):
        return pl.pallas_call(
            forward_end_kernel,
            out_shape=(f32(TILE, CHANS), f32(TILE, CHANS), f32(8, CHANS), message(N_COLS)),
            in_specs=[VMEM] * 3,
            out_specs=(VMEM,) * 4,
            compiler_params=LIMIT,
            name="forward_end",
        )(received, raw, unit)

    def last_end(received, raw, unit):
        spread = pl.pallas_call(
            last_end_kernel,
            out_shape=f32(128, 2, CHANS),
            in_specs=[VMEM] * 3,
            out_specs=VMEM,
            compiler_params=LIMIT,
            name="last_end",
        )(received, raw, unit)
        parts = lax.all_to_all(spread, ("yh", "z", "x", "yl"), 0, 0).reshape(2, 64, 2, CHANS)
        rows = jnp.stack([jnp.sum(parts[:, :, 0], axis=1), parts[:, 0, 1]]).reshape(2, CORE_CHANS)
        rows = in_order(core, rows, lax.ppermute(rows, "core", swap), 1)
        return rows[0], rows[1]

    def send_home(vectors, scalars):
        n = len(vectors)
        rows = jnp.stack(scalars)
        rows = jnp.concatenate([rows, jnp.zeros((8 - len(scalars), CHANS), F32)])
        size = PAIR
        stacked = jnp.stack(vectors)
        for name, at, last in (("yh", yh, False), ("core", core, True)):
            width = stacked.shape[-1]
            kept = lax.dynamic_slice_in_dim(stacked, at * size, size, 1).reshape(n * size, width)
            sent = lax.dynamic_slice_in_dim(stacked, (1 - at) * size, size, 1).reshape(n * size, width)
            arrived = lax.ppermute(jnp.concatenate([sent, rows]), name, swap)
            both = in_order(at, jnp.concatenate([kept, rows]), arrived, 1)
            stacked, rows = both[:-8].reshape(n, size, 2 * width), both[-8:]
            size //= 2
        return [stacked[i] for i in range(n)], [rows[i] for i in range(len(scalars))]

    sends = pl.pallas_call(
        first_kernel,
        out_shape=message(N_COLS, PAIR, CORE_CHANS),
        in_specs=[VMEM],
        out_specs=VMEM,
        compiler_params=LIMIT,
        name="first",
    )(jnp.concatenate([rewards_kept, rewards_sent], axis=1))
    received = lax.all_to_all(sends, COLS, 0, 0)
    received, far_slots, rewards_arrived = lax.optimization_barrier((received, far_slots, rewards_arrived))
    meta = jnp.concatenate([pair_slots, far_slots, places])
    rewards_own = in_order(yh, rewards_kept, rewards_arrived, 0)
    sends, far = first_adjoint(received, own)
    raw, unit, beta_rows, sends = adjoint_end(lax.all_to_all(sends, "z", 0, 0), rewards_own, None)
    far, _ = lax.optimization_barrier((far, sends))
    tiles = pair + [far] + [lax.ppermute(part, "core", swap) for part in (far[:PART], far[PART:])]
    raws, alphas, betas = [raw], [], [beta_rows[0]]
    for iteration in range(ITERS):
        received = forward(lax.all_to_all(sends, "z", 0, 0))
        if iteration == ITERS - 1:
            raws, scalars = send_home(raws, betas + alphas)
            next_square, last_alpha = last_end(received, raw, unit)
        left, right, alpha_rows, sends = forward_end(received, raw, unit)
        raw, unit, beta_rows, sends = adjoint_end(adjoint(lax.all_to_all(sends, COLS, 0, 0)), left, right)
        if iteration < ITERS - 1:
            raws.append(raw)
            alphas.append(alpha_rows[0])
            betas.append(beta_rows[0])
    betas, alphas = scalars[:ITERS] + [jnp.sqrt(next_square + EPS)], scalars[ITERS:] + [last_alpha]

    phibar, rhobar = betas[0], alphas[0]
    direction = [1.0 / alphas[0]]
    estimate = []
    for iteration in range(ITERS):
        beta_val = betas[iteration + 1]
        rho_val = jnp.sqrt(rhobar * rhobar + beta_val * beta_val)
        cosine = rhobar / rho_val
        sine_val = beta_val / rho_val
        phi_val = cosine * phibar
        phibar = sine_val * phibar
        weight = phi_val / rho_val
        estimate = [e + weight * d for e, d in zip(estimate + [0.0], direction)]
        if iteration < ITERS - 1:
            alpha_val = alphas[iteration + 1]
            theta_val = sine_val * alpha_val
            rhobar = -cosine * alpha_val
            direction = [-(theta_val / rho_val) * d for d in direction] + [1.0 / alpha_val]
    total = sum(e[None, :] * w for e, w in zip(estimate, raws))
    return (total, phibar / betas[0])


def solution(mesh):
    fine = Mesh(np.asarray(mesh.devices).reshape(SIZES), AXES)
    rows = ("z", "yh", "core")
    return jax.shard_map(
        shards,
        mesh=fine,
        in_specs=(
            P(AXES, None),
            P(rows, COLS, None, None, None),
            P(rows, COLS, None),
            P(rows, COLS),
        ),
        out_specs=(P(AXES, None), P()),
        check_vma=False,
    )
```
